32 devices in a mesh: shard: 4 (over z), replica: 8 (over y, x, core).
Axes of the slice: x: 2, y: 2, z: 4, core: 2. Of those that a mesh axis runs over, the one named last changes fastest.
Arguments:
- tokens: bfloat16 [8, 3072, 1024], P('replica', 'shard'), may hold values from -6 to 6
- seq_lengths: int32 [8, 6], P('replica'), may hold values from 1 to 1536, as said below
- gain_one: bfloat16 [1024], P('shard'), may hold values from 0.5 to 1.5
- in_weight: bfloat16 [3072, 1024], P('shard'), may hold values from -0.1875 to 0.1875
- conv_weight: bfloat16 [1024, 3], P('shard'), may hold values from -3.5 to 3.5
- out_weight: bfloat16 [1024, 1024], P('shard'), may hold values from -0.1875 to 0.1875
- gain_two: bfloat16 [1024], P('shard'), may hold values from 0.5 to 1.5
- gate_weight: bfloat16 [4608, 1024], P('shard'), may hold values from -0.1875 to 0.1875
- up_weight: bfloat16 [4608, 1024], P('shard'), may hold values from -0.1875 to 0.1875
- down_weight: bfloat16 [1024, 4608], P('shard'), may hold values from -0.09375 to 0.09375
- cotangent: bfloat16 [8, 3072, 1024], P('replica', 'shard'), may hold values from -6 to 6
Outputs:
- block_out: bfloat16 [8, 3072, 1024], P('replica', 'shard')
- input_grad: float32 [8, 3072, 1024], P('replica', 'shard')
- gain_one_grad: float32 [1024], P('shard')
- in_weight_grad: float32 [3072, 1024], P('shard')
- conv_weight_grad: float32 [1024, 3], P('shard')
- out_weight_grad: float32 [1024, 1024], P('shard')
- gain_two_grad: float32 [1024], P('shard')
- gate_weight_grad: float32 [4608, 1024], P('shard')
- up_weight_grad: float32 [4608, 1024], P('shard')
- down_weight_grad: float32 [1024, 4608], P('shard')
The draws below stay inside these ranges and needn't reach their ends.
Inputs may be any that keep to these rules, and one draw needn't show every extreme that they name: `seq_lengths`: in each row the 6 lengths sum to 3072, and the largest is exactly 1536.
All inputs are finite; a program needn't handle non-finite values.
Results may differ from the reference program's by a relative error of at most 0.017.
Values may be sent and summed in bfloat16 or wider, within the bound.
A program may use at most 256 MiB of HBM per device.

```python
import jax
import jax.numpy as jnp
from jax import lax

D = 1024
FF = 4608
KW = 3
NSEQ = 6
GTOK = 3072
MAXLEN = 1536
N_REPLICA = 8


def group_lengths(key, total, longest, count):
    sub_keys = jax.random.split(key, 3)
    pieces = count - 1
    rest = total - longest
    base = rest // pieces
    spare = rest - base * pieces
    spread = max(0, min(base // 2, longest - base - 4))
    pairs = pieces // 2
    shifts = jax.random.randint(sub_keys[0], (pairs,), -spread, spread + 1)
    diffs = jnp.concatenate([shifts, -shifts, jnp.zeros((pieces - 2 * pairs,), jnp.int32)])
    slot_ids = lax_iota(pieces)
    others = base + diffs + jnp.where(slot_ids == pieces - 1, spare, 0)
    others = others[jax.random.permutation(sub_keys[1], pieces)]
    where_long = jax.random.randint(sub_keys[2], (), 0, count)
    all_ids = lax_iota(count)
    source = jnp.clip(jnp.where(all_ids < where_long, all_ids, all_ids - 1), 0, pieces - 1)
    return jnp.where(all_ids == where_long, longest, others[source]).astype(jnp.int32)


def lax_iota(count):
    return jnp.arange(count, dtype=jnp.int32)


def draw_seq_lengths(key, part):
    key = jax.random.fold_in(key, 11)
    row_keys = jax.random.split(key, N_REPLICA)
    return jax.vmap(lambda row_key: group_lengths(row_key, GTOK, MAXLEN, NSEQ))(row_keys)


def steps_of(key, shape, shards, smallest, largest):
    level = 1.0
    for dim, shards_of in shards:
        draws = jax.random.uniform(jax.random.fold_in(jax.random.fold_in(key, 6), dim), (shards_of,), jnp.float32, smallest / len(shards), largest / len(shards))
        level = level * jnp.repeat(jnp.exp(draws), shape[dim] // shards_of).reshape((-1,) + (1,) * (len(shape) - 1 - dim))
    return level


def gaussian(stream_key, dims, scale, reach, cuts=(), held_as=jnp.bfloat16):
    loudness = steps_of(stream_key, dims, cuts, -0.22, 0.18) if cuts else 1.0
    values = jax.random.normal(stream_key, dims, jnp.float32) * scale * loudness
    return jnp.minimum(jnp.maximum(values, -reach), reach).astype(held_as)


def setup_inputs(seed: int = 0) -> dict:
    key_list = jax.random.split(jax.random.key(seed), 12)
    return {
        "tokens": gaussian(key_list[0], (N_REPLICA, GTOK, D), 1.0, 6.0, ((0, 8), (1, 4))),
        "seq_lengths": draw_seq_lengths(jax.random.fold_in(key_list[11], 71), 0),
        "gain_one": jnp.clip(1.0 + 0.1 * jax.random.normal(key_list[2], (D,), jnp.float32), 0.5, 1.5).astype(jnp.bfloat16),
        "in_weight": gaussian(key_list[3], (3 * D, D), D ** -0.5, 0.1875, ((0, 4),)),
        "conv_weight": gaussian(key_list[4], (D, KW), KW ** -0.5, 3.5, ((0, 4),)),
        "out_weight": gaussian(key_list[5], (D, D), D ** -0.5, 0.1875, ((0, 4),)),
        "gain_two": jnp.clip(1.0 + 0.1 * jax.random.normal(key_list[6], (D,), jnp.float32), 0.5, 1.5).astype(jnp.bfloat16),
        "gate_weight": gaussian(key_list[7], (FF, D), D ** -0.5, 0.1875, ((0, 4),)),
        "up_weight": gaussian(key_list[8], (FF, D), D ** -0.5, 0.1875, ((0, 4),)),
        "down_weight": gaussian(key_list[9], (D, FF), FF ** -0.5, 0.09375, ((0, 4),)),
        "cotangent": gaussian(key_list[10], (N_REPLICA, GTOK, D), 1.0, 6.0, ((0, 8), (1, 4))),
    }


NORM_EPS = 1e-05

@jax.custom_vjp
def low(v):
    return lax.optimization_barrier(v.astype(jnp.bfloat16)).astype(jnp.float32)

@jax.custom_vjp
def low_back(v):
    return v

def low_keep(v):
    return (low(v), None)

def low_pass(kept, grad):
    return (grad,)

def back_keep(v):
    return (v, None)

def back_low(kept, grad):
    return (low(grad),)
low.defvjp(low_keep, low_pass)
low_back.defvjp(back_keep, back_low)

def times_rows(left_side, weight):
    return jnp.dot(left_side, weight.T, precision=lax.Precision.HIGHEST)

def starts_of(seq_lens):
    seq_order = lax.iota(jnp.int32, seq_lens.shape[0])
    return lax.optimization_barrier(jnp.sum(jnp.where(seq_order[None, :] < seq_order[:, None], seq_lens[None, :], 0), axis=1)).astype(jnp.int32)

def opens_at(positions, starts):
    return jnp.any(positions[:, None] == starts[None, :], axis=1)

def keep_masks(seq_lens):
    starts = starts_of(seq_lens)
    positions = lax.iota(jnp.int32, GTOK)
    opens_here = opens_at(positions, starts)
    opens_prior = opens_at(positions - 1, starts)
    keep_one = jnp.where(opens_here, 0.0, 1.0).astype(jnp.float32)[:, None]
    keep_two = jnp.where(opens_here | opens_prior, 0.0, 1.0).astype(jnp.float32)[:, None]
    return (keep_one, keep_two)

def lag_rows(values, amount):
    return jnp.concatenate([jnp.zeros((amount, values.shape[1]), values.dtype), values[:-amount]], axis=0)

def layer_block(params, hidden, keep_one, keep_two):
    gain_first, in_full, taps_full, outw_full, gain_second, gate_full, up_full, down_full = params
    model_width = outw_full.shape[0]
    scale_one = lax.rsqrt(lax.optimization_barrier(jnp.mean(hidden * hidden, axis=1, keepdims=True)) + NORM_EPS)
    normed = low(hidden * scale_one * gain_first)
    projected = low_back(times_rows(normed, in_full))
    b_part = projected[:, :model_width]
    c_part = projected[:, model_width:2 * model_width]
    x_part = projected[:, 2 * model_width:]
    gated = low(b_part * x_part)
    conv_out = low_back(taps_full[:, 2] * gated + taps_full[:, 1] * lag_rows(gated, 1) * keep_one + taps_full[:, 0] * lag_rows(gated, 2) * keep_two)
    mixed_in = low(c_part * conv_out)
    branch = low_back(times_rows(mixed_in, outw_full))
    middle = hidden + branch
    scale_two = lax.rsqrt(lax.optimization_barrier(jnp.mean(middle * middle, axis=1, keepdims=True)) + NORM_EPS)
    normed_two = low(middle * scale_two * gain_second)
    gate_val = low_back(times_rows(normed_two, gate_full))
    up_val = low_back(times_rows(normed_two, up_full))
    act_val = low(jax.nn.silu(gate_val) * up_val)
    return middle + times_rows(act_val, down_full)

def reference(tokens, seq_lengths, gain_one, in_weight, conv_weight, out_weight, gain_two, gate_weight, up_weight, down_weight, cotangent):
    params = (gain_one.astype(jnp.float32), in_weight.astype(jnp.float32), conv_weight.astype(jnp.float32), out_weight.astype(jnp.float32), gain_two.astype(jnp.float32), gate_weight.astype(jnp.float32), up_weight.astype(jnp.float32), down_weight.astype(jnp.float32))

    def one_group(running, group_items):
        tok_rows, cot_rows, seq_lens = group_items
        keep_one, keep_two = keep_masks(seq_lens)

        def forward(weights, inputs):
            return layer_block(weights, inputs, keep_one, keep_two)
        result, pullback = jax.vjp(forward, params, tok_rows.astype(jnp.float32))
        weight_grads, input_back = pullback(cot_rows.astype(jnp.float32))
        running = jax.tree.map(jnp.add, running, weight_grads)
        return (running, (result.astype(jnp.bfloat16), input_back))
    zero_grads = jax.tree.map(jnp.zeros_like, params)
    running, (block_out, input_grad) = lax.scan(one_group, zero_grads, (tokens, cotangent, seq_lengths))
    return (block_out, input_grad, running[0], running[1], running[2], running[3], running[4], running[5], running[6], running[7])
```

```python
import jax
import jax.numpy as jnp
from jax import lax
from jax.sharding import PartitionSpec as P

NORM_EPS = 1e-05


def shifted(value, axis, steps):
    count = lax.axis_size(axis)
    initial, last = (max(0, -steps), min(count, count - steps))
    return lax.ppermute(value, axis, [(source, source + steps) for source in range(initial, last)])


def times_rows(left_side, weight):
    return lax.dot_general(
        left_side, weight, (((1,), (1,)), ((), ())), preferred_element_type=jnp.float32
    )


def over_rows(left_side, right_side):
    return lax.dot_general(
        left_side, right_side, (((0,), (0,)), ((), ())), preferred_element_type=jnp.float32
    )


def plain_dot(left_side, weight):
    return jnp.dot(left_side, weight, preferred_element_type=jnp.float32)


def starts_of(seq_lens):
    seq_order = lax.iota(jnp.int32, seq_lens.shape[0])
    return jnp.sum(jnp.where(seq_order[None, :] < seq_order[:, None], seq_lens[None, :], 0), axis=1)


def opens_at(positions, starts):
    return jnp.any(positions[:, None] == starts[None, :], axis=1)


def norm_back(grad_rows, values, scale_val, gain_val):
    weighted = grad_rows * gain_val
    inner_mean = jnp.mean(weighted * values, axis=1, keepdims=True)
    cubed = scale_val * scale_val * scale_val
    return (
        scale_val * weighted - values * cubed * inner_mean,
        jnp.sum(grad_rows * values * scale_val, axis=0),
    )


def bits_of(count):
    return [1 << place for place in range(count.bit_length() - 1)]


def swap(value, axis, bit):
    count = lax.axis_size(axis)
    return lax.ppermute(value, axis, [(source, source ^ bit) for source in range(count)])


def route(order):
    far = [("replica", bit) for bit in bits_of(lax.axis_size("replica"))[1:]]
    if order:
        far = far[::-1]
    return far


def shard_route():
    return [("shard", bit) for bit in bits_of(lax.axis_size("shard"))]


CORE = [("replica", 1)]


def own_bit(axis, bit):
    return (lax.axis_index(axis) // bit) % 2


def place_dims(rows):
    shards, replicas = lax.axis_size("shard"), lax.axis_size("replica")
    depth = len(bits_of(shards)) + len(bits_of(replicas))
    return (2,) * depth, rows // (shards * replicas)


def dim_of(axis, bit, held):
    full = [("shard", b) for b in bits_of(lax.axis_size("shard"))[::-1]]
    full = full + [("replica", b) for b in bits_of(lax.axis_size("replica"))[::-1]]
    return sum(1 for item in full[: full.index((axis, bit))] if item in held)


def spread(block, hops, held):
    held = list(held)
    for axis, bit in hops:
        other = swap(block, axis, bit)
        dim = dim_of(axis, bit, held)
        shape = block.shape[:dim] + (2,) + block.shape[dim:]
        mine = lax.broadcasted_iota(jnp.int32, shape, dim) == own_bit(axis, bit)
        block = jnp.where(mine, jnp.expand_dims(block, dim), jnp.expand_dims(other, dim))
        held.append((axis, bit))
    return block


def gather_rows(block, order):
    replicas = lax.axis_size("replica")
    rows = block.shape[0] // replicas
    piece = lax.dynamic_slice_in_dim(block, lax.axis_index("replica") * rows, rows, 0)
    whole = spread(piece, shard_route() + route(order) + CORE, [])
    return whole.reshape((-1, block.shape[1]))


class Reduction:
    def __init__(self, grad, order):
        dims, rows = place_dims(grad.shape[0])
        self.width = grad.shape[1]
        self.value = grad.astype(jnp.bfloat16).reshape(dims + (rows, self.width))
        self.held = shard_route() + CORE + route(order)
        self.down = CORE + route(order) + shard_route()[::-1]
        self.up = route(1 - order) + CORE

    def live(self):
        return bool(self.down or self.up)

    def step(self):
        if self.down:
            axis, bit = self.down.pop(0)
            self.held.remove((axis, bit))
            dim = dim_of(axis, bit, self.held)
            side = own_bit(axis, bit)
            away = lax.dynamic_index_in_dim(self.value, 1 - side, dim, keepdims=False)
            here = lax.dynamic_index_in_dim(self.value, side, dim, keepdims=False)
            came = swap(away, axis, bit)
            total = here.astype(jnp.float32) + came.astype(jnp.float32)
            self.value = total.astype(jnp.bfloat16)
        elif self.up:
            hop = self.up.pop(0)
            self.value = spread(self.value, [hop], self.held)
            self.held.append(hop)

    def result(self):
        return self.value.reshape((-1, self.width)).astype(jnp.float32)


def tie(values, *reductions):
    out = lax.optimization_barrier(tuple(values) + tuple(one.value for one in reductions))
    for one, value in zip(reductions, out[len(values):]):
        one.value = value
    return out[: len(values)]


def total_of(value):
    for axis, bit in CORE + route(0) + shard_route():
        value = value + swap(value, axis, bit)
    return value


def on_device(
    tokens,
    seq_lengths,
    gain_one,
    in_weight,
    conv_weight,
    out_weight,
    gain_two,
    gate_weight,
    up_weight,
    down_weight,
    cotangent,
):
    own_width = gain_one.shape[0]
    slim = jnp.concatenate([gain_one[None], gain_two[None], conv_weight.T], axis=0)
    slim = spread(slim, shard_route(), [])
    slim = slim.reshape((-1,) + slim.shape[-2:]).swapaxes(0, 1).reshape(slim.shape[-2], -1)
    gain_first, gain_second, taps_full = slim[0], slim[1], slim[2:].T
    in_full = gather_rows(in_weight, 1)
    outw_full = gather_rows(out_weight, 0)
    gate_full = gather_rows(gate_weight, 1)
    up_full = gather_rows(up_weight, 0)
    down_full = gather_rows(down_weight, 0)
    model_width = outw_full.shape[0]
    tok_count = tokens.shape[1]
    hidden = tokens[0].astype(jnp.float32)
    starts = starts_of(seq_lengths[0])
    positions = lax.axis_index("shard") * tok_count - 2 + lax.iota(jnp.int32, tok_count + 4)
    opens_here = opens_at(positions, starts)
    opens_prior = opens_at(positions - 1, starts)
    keep_one = jnp.where(opens_here, 0.0, 1.0).astype(jnp.float32)[:, None]
    keep_two = jnp.where(opens_here | opens_prior, 0.0, 1.0).astype(jnp.float32)[:, None]
    gain_a = gain_first.astype(jnp.float32)
    gain_b = gain_second.astype(jnp.float32)
    conv_taps = taps_full.astype(jnp.float32)
    scale_one = lax.rsqrt(jnp.mean(hidden * hidden, axis=1, keepdims=True) + NORM_EPS)
    normed = (hidden * scale_one * gain_a).astype(jnp.bfloat16)
    projected = times_rows(normed, in_full)
    b_part = projected[:, :model_width]
    c_part = projected[:, model_width : 2 * model_width]
    x_part = projected[:, 2 * model_width :]
    gated = (b_part * x_part).astype(jnp.bfloat16)
    rim_rows = shifted(gated[tok_count - 2 :], "shard", 1)
    extended = jnp.concatenate([rim_rows, gated], axis=0).astype(jnp.float32)
    current = extended[2:]
    lag_one = extended[1 : tok_count + 1] * keep_one[2 : tok_count + 2]
    lag_two = extended[:tok_count] * keep_two[2 : tok_count + 2]
    conv_out = conv_taps[:, 2] * current + conv_taps[:, 1] * lag_one + conv_taps[:, 0] * lag_two
    mixed_in = (c_part * conv_out).astype(jnp.bfloat16)
    middle = hidden + times_rows(mixed_in, outw_full)
    scale_two = lax.rsqrt(jnp.mean(middle * middle, axis=1, keepdims=True) + NORM_EPS)
    normed_two = (middle * scale_two * gain_b).astype(jnp.bfloat16)
    gate_val = times_rows(normed_two, gate_full)
    up_val = times_rows(normed_two, up_full)
    sig_val = jax.nn.sigmoid(gate_val)
    silu_val = gate_val * sig_val
    act_val = (silu_val * up_val).astype(jnp.bfloat16)
    cot_rows = cotangent[0]
    down_wgrad = over_rows(cot_rows, act_val)
    down_red = Reduction(down_wgrad, 0)
    (cot_back,) = tie((cot_rows,), down_red)
    act_back = plain_dot(cot_back, down_full)
    down_red.step()
    gate_back = (act_back * up_val * sig_val * (1.0 + gate_val * (1.0 - sig_val))).astype(
        jnp.bfloat16
    )
    up_back = (act_back * silu_val).astype(jnp.bfloat16)
    gate_back, up_back = tie((gate_back, up_back), down_red)
    down_red.step()
    gate_red = Reduction(over_rows(gate_back, normed_two), 1)
    (up_back,) = tie((up_back,), gate_red)
    gate_red.step()
    up_red = Reduction(over_rows(up_back, normed_two), 0)
    up_back, gate_back = tie((up_back, gate_back), gate_red, up_red)
    gate_red.step()
    up_red.step()
    gate_part = plain_dot(gate_back, gate_full)
    gate_part, up_back = tie((gate_part, up_back), up_red)
    up_red.step()
    normed_two_back = gate_part + plain_dot(up_back, up_full)
    (normed_two_back,) = tie((normed_two_back,), down_red)
    down_red.step()
    middle_back, gain_two_wgrad = norm_back(normed_two_back, middle, scale_two, gain_b)
    middle_back = middle_back + cot_rows.astype(jnp.float32)
    branch_back = middle_back.astype(jnp.bfloat16)
    out_red = Reduction(over_rows(branch_back, mixed_in), 1)
    (branch_back,) = tie((branch_back,), out_red)
    out_red.step()
    mixin_back = plain_dot(branch_back, outw_full)
    cpart_back = mixin_back * conv_out
    conv_back = (mixin_back * c_part).astype(jnp.bfloat16)
    after_rows = shifted(conv_back[:2], "shard", -1)
    ahead_rows = jnp.concatenate([conv_back, after_rows], axis=0).astype(jnp.float32)
    conv_here = ahead_rows[:tok_count]
    taps_wgrad = jnp.stack(
        [
            jnp.sum(conv_here * lag_two, axis=0),
            jnp.sum(conv_here * lag_one, axis=0),
            jnp.sum(conv_here * current, axis=0),
        ],
        axis=1,
    )
    gated_back = (
        conv_taps[:, 2] * conv_here
        + conv_taps[:, 1] * ahead_rows[1 : tok_count + 1] * keep_one[3 : tok_count + 3]
        + conv_taps[:, 0] * ahead_rows[2:] * keep_two[4:]
    )
    proj_back = jnp.concatenate(
        [gated_back * x_part, cpart_back, gated_back * b_part], axis=1
    ).astype(jnp.bfloat16)
    (proj_back,) = tie((proj_back,), out_red, down_red, gate_red)
    out_red.step()
    down_red.step()
    gate_red.step()
    in_red = Reduction(over_rows(proj_back, normed), 1)
    proj_back, act_val = tie((proj_back, act_val), in_red)
    in_red.step()
    normed_back = plain_dot(proj_back, in_full)
    hidden_back, gain_one_wgrad = norm_back(normed_back, hidden, scale_one, gain_a)
    hidden_back = hidden_back + middle_back
    every = [down_red, gate_red, up_red, out_red, in_red]
    (normed_back, act_val) = tie((normed_back, act_val), *every)
    result = middle + times_rows(act_val, down_full)
    while any(one.live() for one in every):
        busy = [one for one in every if one.live()]
        for one in busy:
            one.step()
        tie((), *busy)
    slim_grads = jnp.concatenate([gain_one_wgrad[None], gain_two_wgrad[None], taps_wgrad.T], axis=0)
    slim_grads = total_of(slim_grads)
    slim_grads = lax.dynamic_slice_in_dim(
        slim_grads, lax.axis_index("shard") * own_width, own_width, 1
    )
    owned_parts = (
        slim_grads[0],
        in_red.result(),
        slim_grads[2:].T,
        out_red.result(),
        slim_grads[1],
        gate_red.result(),
        up_red.result(),
        down_red.result(),
    )
    return (
        result.astype(jnp.bfloat16)[None],
        hidden_back[None],
        owned_parts[0],
        owned_parts[1],
        owned_parts[2],
        owned_parts[3],
        owned_parts[4],
        owned_parts[5],
        owned_parts[6],
        owned_parts[7],
    )


def solution(mesh):
    return jax.shard_map(
        on_device,
        mesh=mesh,
        in_specs=(
            P("replica", "shard", None),
            P("replica", None),
            P("shard"),
            P("shard", None),
            P("shard", None),
            P("shard", None),
            P("shard"),
            P("shard", None),
            P("shard", None),
            P("shard", None),
            P("replica", "shard", None),
        ),
        out_specs=(
            P("replica", "shard", None),
            P("replica", "shard", None),
            P("shard"),
            P("shard", None),
            P("shard", None),
            P("shard", None),
            P("shard"),
            P("shard", None),
            P("shard", None),
            P("shard", None),
        ),
        check_vma=False,
    )
```

```python
import jax
import jax.numpy as jnp
from jax import lax
from jax.sharding import PartitionSpec as P

NORM_EPS = 1e-05


def shifted(value, axis, steps):
    count = lax.axis_size(axis)
    initial, last = (max(0, -steps), min(count, count - steps))
    return lax.ppermute(value, axis, [(source, source + steps) for source in range(initial, last)])


def times_rows(left_side, weight):
    return lax.dot_general(
        left_side, weight, (((1,), (1,)), ((), ())), preferred_element_type=jnp.float32
    )


def over_rows(left_side, right_side):
    return lax.dot_general(
        left_side, right_side, (((0,), (0,)), ((), ())), preferred_element_type=jnp.float32
    )


def plain_dot(left_side, weight):
    return jnp.dot(left_side, weight, preferred_element_type=jnp.float32)


def starts_of(seq_lens):
    seq_order = lax.iota(jnp.int32, seq_lens.shape[0])
    return jnp.sum(jnp.where(seq_order[None, :] < seq_order[:, None], seq_lens[None, :], 0), axis=1)


def opens_at(positions, starts):
    return jnp.any(positions[:, None] == starts[None, :], axis=1)


def norm_back(grad_rows, values, scale_val, gain_val):
    weighted = grad_rows * gain_val
    inner_mean = jnp.mean(weighted * values, axis=1, keepdims=True)
    cubed = scale_val * scale_val * scale_val
    return (
        scale_val * weighted - values * cubed * inner_mean,
        jnp.sum(grad_rows * values * scale_val, axis=0),
    )


def bits_of(count):
    return [1 << place for place in range(count.bit_length() - 1)]


def swap(value, axis, bit):
    count = lax.axis_size(axis)
    return lax.ppermute(value, axis, [(source, source ^ bit) for source in range(count)])


def route(order):
    far = [("replica", bit) for bit in bits_of(lax.axis_size("replica"))[1:]]
    if order:
        far = far[::-1]
    return far


def shard_route():
    return [("shard", bit) for bit in bits_of(lax.axis_size("shard"))]


CORE = [("replica", 1)]


def own_bit(axis, bit):
    return (lax.axis_index(axis) // bit) % 2


def place_dims(rows):
    shards, replicas = lax.axis_size("shard"), lax.axis_size("replica")
    depth = len(bits_of(shards)) + len(bits_of(replicas))
    return (2,) * depth, rows // (shards * replicas)


def dim_of(axis, bit, held):
    full = [("shard", b) for b in bits_of(lax.axis_size("shard"))[::-1]]
    full = full + [("replica", b) for b in bits_of(lax.axis_size("replica"))[::-1]]
    return sum(1 for item in full[: full.index((axis, bit))] if item in held)


def spread(block, hops, held):
    held = list(held)
    for axis, bit in hops:
        other = swap(block, axis, bit)
        dim = dim_of(axis, bit, held)
        shape = block.shape[:dim] + (2,) + block.shape[dim:]
        mine = lax.broadcasted_iota(jnp.int32, shape, dim) == own_bit(axis, bit)
        block = jnp.where(mine, jnp.expand_dims(block, dim), jnp.expand_dims(other, dim))
        held.append((axis, bit))
    return block


def halved(value):
    half = value.shape[-2] // 2
    return [value[..., :half, :], value[..., half:, :]]


def joined(parts):
    return jnp.concatenate(parts, axis=-2)


class Gather:
    def __init__(self, block):
        replicas = lax.axis_size("replica")
        rows = block.shape[0] // replicas
        self.value = lax.dynamic_slice_in_dim(
            block, lax.axis_index("replica") * rows, rows, 0
        )
        self.width = block.shape[1]
        self.held = []
        self.near, self.orders, self.last = shard_route(), [route(0), route(1)], CORE
        self.parts = None

    def live(self):
        return bool(self.near or self.orders[0] or self.last)

    def step(self):
        if self.near:
            hop = self.near.pop(0)
            self.value = spread(self.value, [hop], self.held)
            self.held.append(hop)
        elif self.orders[0]:
            if self.parts is None:
                self.parts = [(part, list(self.held)) for part in halved(self.value)]
            moved = []
            for (part, held), order in zip(self.parts, self.orders):
                hop = order.pop(0)
                moved.append((spread(part, [hop], held), held + [hop]))
            self.parts = moved
            if not self.orders[0]:
                self.value = joined([part for part, _ in moved])
                self.held = moved[0][1]
                self.parts = None
        elif self.last:
            self.value = spread(self.value, self.last, self.held)
            self.last = []

    def values(self):
        return [self.value] if self.parts is None else [part for part, _ in self.parts]

    def put(self, values):
        if self.parts is None:
            self.value = values[0]
        else:
            self.parts = [(new, held) for new, (_, held) in zip(values, self.parts)]

    def result(self):
        return self.value.reshape((-1, self.width))


def fold(value, hop, held):
    axis, bit = hop
    held = [item for item in held if item != hop]
    dim = dim_of(axis, bit, held)
    side = own_bit(axis, bit)
    away = lax.dynamic_index_in_dim(value, 1 - side, dim, keepdims=False)
    here = lax.dynamic_index_in_dim(value, side, dim, keepdims=False)
    came = swap(away, axis, bit)
    total = here.astype(jnp.float32) + came.astype(jnp.float32)
    return total.astype(jnp.bfloat16), held


class Reduction:
    def __init__(self, grad):
        dims, rows = place_dims(grad.shape[0])
        self.width = grad.shape[1]
        self.value = grad.astype(jnp.bfloat16).reshape(dims + (rows, self.width))
        self.held = shard_route() + CORE + route(0)
        self.core, self.orders, self.near = CORE, [route(0), route(1)], shard_route()[::-1]
        self.parts = None
        self.back = None

    def live(self):
        return self.back is None or self.back.live()

    def step(self):
        if self.back is not None:
            self.back.step()
        elif self.core:
            self.value, self.held = fold(self.value, self.core[0], self.held)
            self.core = []
        elif self.orders[0]:
            if self.parts is None:
                self.parts = [(part, self.held) for part in halved(self.value)]
            self.parts = [
                fold(part, order.pop(0), held)
                for (part, held), order in zip(self.parts, self.orders)
            ]
            if not self.orders[0]:
                self.value, self.held = joined([part for part, _ in self.parts]), self.parts[0][1]
                self.parts = None
        elif self.near:
            self.value, self.held = fold(self.value, self.near.pop(0), self.held)
            if not self.near:
                self.back = Gather.__new__(Gather)
                self.back.value, self.back.width, self.back.held = self.value, self.width, []
                self.back.near, self.back.orders = [], [route(0), route(1)]
                self.back.last, self.back.parts = CORE, None

    def values(self):
        if self.back is not None:
            return self.back.values()
        return [self.value] if self.parts is None else [part for part, _ in self.parts]

    def put(self, values):
        if self.back is not None:
            self.back.put(values)
        elif self.parts is None:
            self.value = values[0]
        else:
            self.parts = [(new, held) for new, (_, held) in zip(values, self.parts)]

    def result(self):
        return self.back.result().astype(jnp.float32)


def tie(values, *movers):
    moving = [one.values() for one in movers]
    out = lax.optimization_barrier((tuple(values), moving))
    for one, new in zip(movers, out[1]):
        one.put(new)
    return out[0]


def total_of(value):
    for axis, bit in CORE + route(0) + shard_route():
        value = value + swap(value, axis, bit)
    return value


def on_device(
    tokens,
    seq_lengths,
    gain_one,
    in_weight,
    conv_weight,
    out_weight,
    gain_two,
    gate_weight,
    up_weight,
    down_weight,
    cotangent,
):
    own_width = gain_one.shape[0]
    slim = jnp.concatenate([gain_one[None], gain_two[None], conv_weight.T], axis=0)
    slim = spread(slim, shard_route(), [])
    slim = slim.reshape((-1,) + slim.shape[-2:]).swapaxes(0, 1).reshape(slim.shape[-2], -1)
    gain_first, gain_second, taps_full = slim[0], slim[1], slim[2:].T
    gathers = [Gather(w) for w in (in_weight, out_weight, gate_weight, up_weight, down_weight)]
    delays = [0, 0, 1, 2, 3]
    turn = 0
    while any(one.live() for one in gathers):
        busy = [one for one, delay in zip(gathers, delays) if one.live() and turn >= delay]
        for one in busy:
            one.step()
        tie((), *busy)
        turn += 1
    in_full, outw_full, gate_full, up_full, down_full = [one.result() for one in gathers]
    model_width = outw_full.shape[0]
    tok_count = tokens.shape[1]
    hidden = tokens[0].astype(jnp.float32)
    starts = starts_of(seq_lengths[0])
    positions = lax.axis_index("shard") * tok_count - 2 + lax.iota(jnp.int32, tok_count + 4)
    opens_here = opens_at(positions, starts)
    opens_prior = opens_at(positions - 1, starts)
    keep_one = jnp.where(opens_here, 0.0, 1.0).astype(jnp.float32)[:, None]
    keep_two = jnp.where(opens_here | opens_prior, 0.0, 1.0).astype(jnp.float32)[:, None]
    gain_a = gain_first.astype(jnp.float32)
    gain_b = gain_second.astype(jnp.float32)
    conv_taps = taps_full.astype(jnp.float32)
    scale_one = lax.rsqrt(jnp.mean(hidden * hidden, axis=1, keepdims=True) + NORM_EPS)
    normed = (hidden * scale_one * gain_a).astype(jnp.bfloat16)
    projected = times_rows(normed, in_full)
    b_part = projected[:, :model_width]
    c_part = projected[:, model_width : 2 * model_width]
    x_part = projected[:, 2 * model_width :]
    gated = (b_part * x_part).astype(jnp.bfloat16)
    rim_rows = shifted(gated[tok_count - 2 :], "shard", 1)
    extended = jnp.concatenate([rim_rows, gated], axis=0).astype(jnp.float32)
    current = extended[2:]
    lag_one = extended[1 : tok_count + 1] * keep_one[2 : tok_count + 2]
    lag_two = extended[:tok_count] * keep_two[2 : tok_count + 2]
    conv_out = conv_taps[:, 2] * current + conv_taps[:, 1] * lag_one + conv_taps[:, 0] * lag_two
    mixed_in = (c_part * conv_out).astype(jnp.bfloat16)
    middle = hidden + times_rows(mixed_in, outw_full)
    scale_two = lax.rsqrt(jnp.mean(middle * middle, axis=1, keepdims=True) + NORM_EPS)
    normed_two = (middle * scale_two * gain_b).astype(jnp.bfloat16)
    gate_val = times_rows(normed_two, gate_full)
    up_val = times_rows(normed_two, up_full)
    sig_val = jax.nn.sigmoid(gate_val)
    silu_val = gate_val * sig_val
    act_val = (silu_val * up_val).astype(jnp.bfloat16)
    cot_rows = cotangent[0]
    down_wgrad = over_rows(cot_rows, act_val)
    down_red = Reduction(down_wgrad)
    (cot_back,) = tie((cot_rows,), down_red)
    act_back = plain_dot(cot_back, down_full)
    down_red.step()
    gate_back = (act_back * up_val * sig_val * (1.0 + gate_val * (1.0 - sig_val))).astype(
        jnp.bfloat16
    )
    up_back = (act_back * silu_val).astype(jnp.bfloat16)
    gate_back, up_back = tie((gate_back, up_back), down_red)
    down_red.step()
    gate_red = Reduction(over_rows(gate_back, normed_two))
    (up_back,) = tie((up_back,), gate_red)
    gate_red.step()
    up_red = Reduction(over_rows(up_back, normed_two))
    up_back, gate_back = tie((up_back, gate_back), gate_red, up_red)
    gate_red.step()
    up_red.step()
    gate_part = plain_dot(gate_back, gate_full)
    gate_part, up_back = tie((gate_part, up_back), up_red)
    up_red.step()
    normed_two_back = gate_part + plain_dot(up_back, up_full)
    (normed_two_back,) = tie((normed_two_back,), down_red)
    down_red.step()
    middle_back, gain_two_wgrad = norm_back(normed_two_back, middle, scale_two, gain_b)
    middle_back = middle_back + cot_rows.astype(jnp.float32)
    branch_back = middle_back.astype(jnp.bfloat16)
    out_red = Reduction(over_rows(branch_back, mixed_in))
    (branch_back,) = tie((branch_back,), out_red)
    out_red.step()
    mixin_back = plain_dot(branch_back, outw_full)
    cpart_back = mixin_back * conv_out
    conv_back = (mixin_back * c_part).astype(jnp.bfloat16)
    after_rows = shifted(conv_back[:2], "shard", -1)
    ahead_rows = jnp.concatenate([conv_back, after_rows], axis=0).astype(jnp.float32)
    conv_here = ahead_rows[:tok_count]
    taps_wgrad = jnp.stack(
        [
            jnp.sum(conv_here * lag_two, axis=0),
            jnp.sum(conv_here * lag_one, axis=0),
            jnp.sum(conv_here * current, axis=0),
        ],
        axis=1,
    )
    gated_back = (
        conv_taps[:, 2] * conv_here
        + conv_taps[:, 1] * ahead_rows[1 : tok_count + 1] * keep_one[3 : tok_count + 3]
        + conv_taps[:, 0] * ahead_rows[2:] * keep_two[4:]
    )
    proj_back = jnp.concatenate(
        [gated_back * x_part, cpart_back, gated_back * b_part], axis=1
    ).astype(jnp.bfloat16)
    (proj_back,) = tie((proj_back,), out_red, down_red, gate_red)
    out_red.step()
    down_red.step()
    gate_red.step()
    in_red = Reduction(over_rows(proj_back, normed))
    proj_back, act_val = tie((proj_back, act_val), in_red)
    in_red.step()
    normed_back = plain_dot(proj_back, in_full)
    hidden_back, gain_one_wgrad = norm_back(normed_back, hidden, scale_one, gain_a)
    hidden_back = hidden_back + middle_back
    every = [down_red, gate_red, up_red, out_red, in_red]
    (normed_back, act_val) = tie((normed_back, act_val), *every)
    result = middle + times_rows(act_val, down_full)
    while any(one.live() for one in every):
        busy = [one for one in every if one.live()]
        for one in busy:
            one.step()
        tie((), *busy)
    slim_grads = jnp.concatenate([gain_one_wgrad[None], gain_two_wgrad[None], taps_wgrad.T], axis=0)
    slim_grads = total_of(slim_grads)
    slim_grads = lax.dynamic_slice_in_dim(
        slim_grads, lax.axis_index("shard") * own_width, own_width, 1
    )
    owned_parts = (
        slim_grads[0],
        in_red.result(),
        slim_grads[2:].T,
        out_red.result(),
        slim_grads[1],
        gate_red.result(),
        up_red.result(),
        down_red.result(),
    )
    return (
        result.astype(jnp.bfloat16)[None],
        hidden_back[None],
        owned_parts[0],
        owned_parts[1],
        owned_parts[2],
        owned_parts[3],
        owned_parts[4],
        owned_parts[5],
        owned_parts[6],
        owned_parts[7],
    )


def solution(mesh):
    return jax.shard_map(
        on_device,
        mesh=mesh,
        in_specs=(
            P("replica", "shard", None),
            P("replica", None),
            P("shard"),
            P("shard", None),
            P("shard", None),
            P("shard", None),
            P("shard"),
            P("shard", None),
            P("shard", None),
            P("shard", None),
            P("replica", "shard", None),
        ),
        out_specs=(
            P("replica", "shard", None),
            P("replica", "shard", None),
            P("shard"),
            P("shard", None),
            P("shard", None),
            P("shard", None),
            P("shard"),
            P("shard", None),
            P("shard", None),
            P("shard", None),
        ),
        check_vma=False,
    )
```
